512 devices in a mesh: seq: 64 (over z, y_lo, core), head: 8 (over x, y_hi).
Axes of the slice: x: 4, y: 4 (y_hi: 2, y_lo: 2; y = y_hi * 2 + y_lo), z: 16, core: 2. Of those that a mesh axis runs over, the one named last changes fastest.
Arguments:
- queries: bfloat16 [32768, 4096], P(('seq', 'head')), may hold values from -64 to 64
- keys: bfloat16 [32768, 1024], P(('seq', 'head')), may hold values from -6 to 6
- values: bfloat16 [32768, 1024], P(('seq', 'head')), may hold values from -6 to 6
- level_bias: float32 [32, 6], P('head'), may hold values from -1 to 2
- anchor_bias: float32 [32], P('head'), may hold values from 1 to 4
- partners: int32 [64, 6], P('seq'), may hold values from 0 to 63, as said below
- anchor_positions: int32 [64], replicated, may hold values from 0 to 32767, as said below
Outputs:
- attended: bfloat16 [32768, 4096], P(('seq', 'head'))
The draws below stay inside these ranges and needn't reach their ends.
Inputs may be any that keep to these rules, and one draw needn't show every extreme that they name: `partners`: row b holds b XOR 2**j once for each j of 0 to 5, in an order drawn for each block. `anchor_positions`: distinct positions.
All inputs are finite; a program needn't handle non-finite values.
Results may differ from the reference program's by a relative error of at most 0.0045.
Values may be sent and summed in bfloat16 or wider, within the bound.
No kernel may reach another device: no remote copies, remote signals or barrier semaphores. Data moves between devices by JAX's collectives and lax.ppermute only.
A program may use at most 128 MiB of HBM per device.

```python
import math
import jax
import jax.numpy as jnp
from jax import lax

QH = 32
KVH = 8
HD = 128
TOK_DEV = 512
NGLOB = 64
BLOCKS = 64
LEVELS = 6
TOKENS = 32768


def shared_keys(key):
    base_key = jax.random.fold_in(key, 7)
    drawn = jnp.clip(jax.random.normal(base_key, (TOKENS, KVH * HD), jnp.float32), -6.0, 6.0)
    return drawn


def draw_keys(key, part):
    drawn = shared_keys(key)
    return drawn.astype(jnp.bfloat16)


def draw_queries(key, part):
    noise_key = jax.random.fold_in(key, 13)
    result = jnp.clip(2.0 * jax.random.normal(noise_key, (TOKENS, QH * HD), jnp.float32), -8.0, 8.0)
    return result.astype(jnp.bfloat16)


def draw_partners(key, part):

    def one_block(block):
        order_bits = jax.random.permutation(jax.random.fold_in(key, block), LEVELS)
        return jnp.bitwise_xor(block, jnp.left_shift(1, order_bits)).astype(jnp.int32)
    return jax.vmap(one_block)(jnp.arange(BLOCKS, dtype=jnp.int32))


def draw_anchor_positions(key, part):
    return jax.random.permutation(jax.random.fold_in(key, 5), TOKENS)[:NGLOB].astype(jnp.int32)


def block_levels(stream_key, dims, split, smallest, largest):
    factor_of, own = 1.0, jax.random.fold_in(stream_key, 6)
    for axis_at, shards_of in split:
        draws = jnp.exp(jax.random.uniform(jax.random.fold_in(own, axis_at), (shards_of,), jnp.float32, smallest / len(split), largest / len(split)))
        factor_of = factor_of * jnp.repeat(draws, dims[axis_at] // shards_of).reshape([-1 if axis == axis_at else 1 for axis in range(len(dims))])
    return factor_of


def scatter_about(stream_key, extent, scale, most, split=(), kind=jnp.bfloat16):
    gain = block_levels(stream_key, extent, split, -0.22, 0.18) if split else 1.0
    values = jax.random.normal(stream_key, extent, jnp.float32) * scale * gain
    return jnp.minimum(jnp.maximum(values, -most), most).astype(kind)


def setup_inputs(seed: int = 0) -> dict:
    arg_keys = jax.random.split(jax.random.key(seed), 8)
    queries = draw_queries(jax.random.fold_in(arg_keys[7], 71), 0)
    keys = draw_keys(jax.random.fold_in(arg_keys[7], 71), 0)
    values = scatter_about(arg_keys[2], (TOKENS, KVH * HD), 1.0, 6.0, ((0, 512),))
    level_bias = jnp.clip(-1.0 + 3.0 * jax.random.uniform(arg_keys[3], (QH, LEVELS), jnp.float32) ** block_levels(arg_keys[3], (QH, LEVELS), ((0, 8),), -0.2, 0.2), -1.0, 2.0)
    anchor_bias = jnp.clip(jnp.exp(math.log(4.0) - 1.3862944 * jax.random.uniform(arg_keys[4], (QH,), jnp.float32) ** block_levels(arg_keys[4], (QH,), ((0, 8),), -0.2, 0.2)), 1.0, 4.0)
    partners = draw_partners(jax.random.fold_in(arg_keys[7], 71), 0)
    anchor_positions = draw_anchor_positions(jax.random.fold_in(arg_keys[7], 71), 0)
    return dict(queries=queries, keys=keys, values=values, level_bias=level_bias, anchor_bias=anchor_bias, partners=partners, anchor_positions=anchor_positions)


def reference(queries, keys, values, level_bias, anchor_bias, partners, anchor_positions):
    group_size = QH // KVH
    score_scale = HD ** -0.5
    anchor_keys = keys[anchor_positions]
    anchor_vals = values[anchor_positions]
    pieces = [jnp.zeros((QH, TOK_DEV), jnp.float32)]
    for level in range(LEVELS):
        pieces.append(jnp.broadcast_to(level_bias[:, level:level + 1], (QH, TOK_DEV)))
    pieces.append(jnp.broadcast_to(anchor_bias[:, None], (QH, NGLOB)))
    key_bias = jnp.concatenate(pieces, axis=1).reshape(KVH, group_size, -1)

    def attend_block(block):
        start = (block * TOK_DEV).astype(jnp.int32)
        query_heads = lax.dynamic_slice_in_dim(queries, start, TOK_DEV, 0).reshape(TOK_DEV, KVH, group_size, HD)
        key_list = [lax.dynamic_slice_in_dim(keys, start, TOK_DEV, 0)]
        value_list = [lax.dynamic_slice_in_dim(values, start, TOK_DEV, 0)]
        for level in range(LEVELS):
            other = (partners[block, level] * TOK_DEV).astype(jnp.int32)
            key_list.append(lax.dynamic_slice_in_dim(keys, other, TOK_DEV, 0))
            value_list.append(lax.dynamic_slice_in_dim(values, other, TOK_DEV, 0))
        key_rows = jnp.concatenate(key_list + [anchor_keys], axis=0).reshape(-1, KVH, HD)
        value_rows = jnp.concatenate(value_list + [anchor_vals], axis=0).reshape(-1, KVH, HD)
        scores = jnp.einsum("tkgd,skd->kgts", query_heads.astype(jnp.float32), key_rows.astype(jnp.float32))
        scores = scores * score_scale + key_bias[:, :, None, :]
        row_max = jnp.max(scores, axis=-1, keepdims=True)
        weights = jnp.exp(scores - row_max)
        denominator = jnp.sum(weights, axis=-1)
        rounded = lax.optimization_barrier(weights.astype(jnp.bfloat16)).astype(jnp.float32)
        numerator = jnp.einsum("kgts,skd->kgtd", rounded, value_rows.astype(jnp.float32))
        result = numerator / denominator[..., None]
        return result.transpose(2, 0, 1, 3).reshape(TOK_DEV, QH * HD).astype(jnp.bfloat16)

    blocks_out = lax.map(attend_block, jnp.arange(BLOCKS, dtype=jnp.int32))
    return blocks_out.reshape(TOKENS, QH * HD)
```

```python
import functools
import math

import jax
import jax.numpy as jnp
from jax import lax
from jax.experimental import pallas as pl
from jax.experimental.pallas import tpu as pltpu
from jax.sharding import PartitionSpec as P

HD = 128
LOG2E = math.log2(math.e)


def swap(value, bit):
    return lax.ppermute(value, "seq", [(i, i ^ (1 << bit)) for i in range(lax.axis_size("seq"))])


def attend_kernel(count, first, final, bias_ref, q_ref, *refs):
    kv_refs, refs = refs[:count], refs[count:]
    if not first:
        acc_in, ml_in, refs = refs[0], refs[1], refs[2:]
    head = pl.program_id(0)
    scale = HD**-0.5 * LOG2E
    rows = q_ref.shape[0]
    tile = 256
    for start in range(0, rows, tile):
        part = pl.ds(start, tile)
        query = q_ref[part, :]
        scores, top = [], None
        for j in range(count):
            s = lax.dot_general(
                query, kv_refs[j][:, :HD], (((1,), (1,)), ((), ())), preferred_element_type=jnp.float32
            )
            bias = bias_ref[j, head] * LOG2E
            most = jnp.max(s, axis=-1, keepdims=True) * scale + bias
            top = most if top is None else jnp.maximum(top, most)
            scores.append((s, bias))
        if not first:
            old_top = ml_in[0, part, 0:1]
            top = jnp.maximum(top, old_top)
        total = None
        for j in range(count):
            s, bias = scores[j]
            weights = jnp.exp2(s * scale - (top - bias)).astype(jnp.bfloat16)
            value = kv_refs[j][:, HD:]
            widened = jnp.concatenate([value, jnp.ones_like(value)], axis=1)
            update = jnp.dot(weights, widened, preferred_element_type=jnp.float32)
            total = update if total is None else total + update
        acc, summed = total[:, :HD], total[:, HD:]
        if not first:
            rescale = jnp.exp2(old_top - top)
            acc = acc + acc_in[0, part, :] * rescale
            summed = summed + ml_in[0, part, 1:2] * rescale
        if final:
            refs[0][part, :] = (acc / summed).astype(jnp.bfloat16)
        else:
            refs[0][0, part, :] = acc
            refs[1][0, part, 0:1] = top
            refs[1][0, part, 1:2] = summed[:, 0:1]


def attend(state, queries, blocks, biases, final=False):
    rows, width = queries.shape
    heads = biases.shape[1]
    count, first = len(blocks), state is None
    acc_spec = pl.BlockSpec((1, rows, HD), lambda h: (h, 0, 0))
    ml_spec = pl.BlockSpec((1, rows, 2), lambda h: (h, 0, 0))
    q_spec = pl.BlockSpec((rows, HD), lambda h: (0, h))
    in_specs = [pl.BlockSpec(memory_space=pltpu.SMEM), q_spec]
    in_specs += [pl.BlockSpec(b.shape, lambda h: (0, 0)) for b in blocks]
    args = [biases, queries, *blocks]
    if not first:
        in_specs += [acc_spec, ml_spec]
        args += list(state)
    if final:
        out_shape = jax.ShapeDtypeStruct((rows, heads * HD), jnp.bfloat16)
        out_specs = q_spec
    else:
        out_shape = (
            jax.ShapeDtypeStruct((heads, rows, HD), jnp.float32),
            jax.ShapeDtypeStruct((heads, rows, 2), jnp.float32),
        )
        out_specs = (acc_spec, ml_spec)
    return pl.pallas_call(
        functools.partial(attend_kernel, count, first, final),
        grid=(heads,),
        in_specs=in_specs,
        out_specs=out_specs,
        out_shape=out_shape,
        compiler_params=pltpu.CompilerParams(vmem_limit_bytes=48 * 1024 * 1024),
    )(*args)


def on_device(queries, keys, values, level_bias, anchor_bias, partners, anchor_positions):
    tokens = queries.shape[0]
    shards = lax.axis_size("head")
    block_index = lax.axis_index("seq")
    bits = lax.axis_size("seq").bit_length() - 1

    def by_head(array):
        return array.reshape(tokens, shards, -1).transpose(1, 0, 2)

    def to_heads(array):
        gathered = lax.all_to_all(array, "head", split_axis=0, concat_axis=0, tiled=True)
        return gathered.reshape(shards * tokens, -1)

    kv_shard = jnp.concatenate([by_head(keys), by_head(values)], axis=2)
    far_shard = swap(kv_shard, bits - 1)
    qkv = to_heads(jnp.concatenate([by_head(queries), kv_shard], axis=2))
    q_width = queries.shape[1] // shards
    q, kv = qkv[:, :q_width], qkv[:, q_width:]

    token_index = block_index * kv.shape[0] + jnp.arange(kv.shape[0], dtype=jnp.int32)
    selector = (anchor_positions[:, None] == token_index[None, :]).astype(jnp.bfloat16)
    anchors = jnp.dot(selector, kv, preferred_element_type=jnp.float32).astype(jnp.bfloat16)

    others = [swap(kv, bit) for bit in range(bits - 1)]
    for bit in range(bits):
        anchors = anchors + swap(anchors, bit)
    far = to_heads(far_shard)

    block_bias = [jnp.zeros_like(anchor_bias)]
    for bit in range(bits):
        chosen = (partners[0] == jnp.bitwise_xor(block_index, 1 << bit)).astype(jnp.float32)
        block_bias.append(jnp.sum(level_bias * chosen[None, :], axis=1))
    block_bias.append(anchor_bias)
    bias = jnp.stack(block_bias)

    state = attend(None, q, [kv, others[0], others[1]], bias[0:3])
    state = attend(state, q, [others[2], others[3]], bias[3:5])
    state = attend(state, q, [far], bias[6:7])
    result = attend(state, q, [others[4], anchors], jnp.stack([bias[5], bias[7]]), final=True)
    return lax.all_to_all(result, "head", split_axis=0, concat_axis=1, tiled=True)


def solution(mesh):
    in_specs = (
        P(("seq", "head"), None),
        P(("seq", "head"), None),
        P(("seq", "head"), None),
        P("head", None),
        P("head"),
        P("seq", None),
        P(),
    )
    out_specs = P(("seq", "head"), None)
    return jax.shard_map(
        on_device, mesh=mesh, in_specs=in_specs, out_specs=out_specs, check_vma=False
    )
```

```python
import functools
import math

import jax
import jax.numpy as jnp
from jax import lax
from jax.experimental import pallas as pl
from jax.experimental.pallas import tpu as pltpu
from jax.sharding import PartitionSpec as P

HD = 128
LOG2E = math.log2(math.e)


def swap(value, bit):
    return lax.ppermute(value, "seq", [(i, i ^ bit) for i in range(lax.axis_size("seq"))])


def attend_kernel(count, first, final, bias_ref, q_ref, *refs):
    k_refs, v_refs, refs = refs[: 2 * count : 2], refs[1 : 2 * count : 2], refs[2 * count :]
    if not first:
        acc_in, stat_in, refs = refs[0], refs[1], refs[2:]
    scale = HD**-0.5 * LOG2E
    rows, heads = q_ref.shape[0], q_ref.shape[1] // HD
    tile = 256
    for head in range(heads):
        for start in range(0, rows, tile):
            part, cols = pl.ds(start, tile), pl.ds(head * HD, HD)
            query = q_ref[part, cols]
            scores, top = [], None
            for j in range(count):
                s = lax.dot_general(
                    query, k_refs[j][...], (((1,), (1,)), ((), ())), preferred_element_type=jnp.float32
                )
                bias = bias_ref[j, head] * LOG2E
                most = jnp.max(s, axis=-1, keepdims=True) * scale + bias
                top = most if top is None else jnp.maximum(top, most)
                scores.append((s, bias))
            if first:
                top = jnp.broadcast_to(top, (tile, HD))
            else:
                old_top = jnp.broadcast_to(stat_in[part, head : head + 1], (tile, HD))
                top = jnp.maximum(old_top, top)
            total = None
            for j in range(count):
                s, bias = scores[j]
                weights = jnp.exp2(s * scale - (top[:, :1] - bias)).astype(jnp.bfloat16)
                value = v_refs[j][...]
                widened = jnp.concatenate([value, jnp.ones_like(value)], axis=1)
                update = jnp.dot(weights, widened, preferred_element_type=jnp.float32)
                total = update if total is None else total + update
            acc, summed = total[:, :HD], total[:, HD:]
            if not first:
                rescale = jnp.exp2(old_top - top)
                acc = acc + acc_in[part, cols] * rescale
                old_sum = stat_in[part, heads + head : heads + head + 1]
                summed = summed + jnp.broadcast_to(old_sum, (tile, HD)) * rescale
            if final:
                refs[0][part, cols] = (acc / summed).astype(jnp.bfloat16)
            else:
                refs[0][part, cols] = acc
                refs[1][part, head : head + 1] = top[:, :1]
                refs[1][part, heads + head : heads + head + 1] = summed[:, :1]


def attend(state, queries, blocks, biases, final=False):
    rows, heads = queries.shape[0], biases.shape[1]
    width, count, first = heads * HD, len(blocks), state is None
    steps = 2

    def by_rows(columns):
        return pl.BlockSpec((rows // steps, columns), lambda i: (i, 0))

    def columns_at(size, place):
        return pl.BlockSpec((size, HD), lambda i: (0, place))

    state_specs = (by_rows(width), by_rows(2 * heads))
    in_specs = [pl.BlockSpec(memory_space=pltpu.SMEM), by_rows(width)]
    args = [biases, queries]
    for size, key_array, key_place, value_array, value_place in blocks:
        in_specs += [columns_at(size, key_place), columns_at(size, value_place)]
        args += [key_array, value_array]
    if not first:
        in_specs += state_specs
        args += state
    if final:
        out_shape, out_specs = jax.ShapeDtypeStruct((rows, width), jnp.bfloat16), by_rows(width)
    else:
        out_shape = tuple(jax.ShapeDtypeStruct((rows, n), jnp.float32) for n in (width, 2 * heads))
        out_specs = state_specs
    return pl.pallas_call(
        functools.partial(attend_kernel, count, first, final),
        grid=(steps,),
        in_specs=in_specs,
        out_specs=out_specs,
        out_shape=out_shape,
        compiler_params=pltpu.CompilerParams(vmem_limit_bytes=24 * 1024 * 1024),
    )(*args)


def on_device(queries, keys, values, level_bias, anchor_bias, partners, anchor_positions):
    tokens = queries.shape[0]
    shards = lax.axis_size("head")
    blocks = lax.axis_size("seq")
    block_index = lax.axis_index("seq")
    bits = blocks.bit_length() - 1
    after = lax.optimization_barrier
    places = queries.shape[1] // shards // HD
    rows = shards * tokens

    def by_head(array):
        return array.reshape(tokens, shards, -1).transpose(1, 0, 2)

    def to_heads(array):
        gathered = lax.all_to_all(array, "head", split_axis=0, concat_axis=0, tiled=True)
        return gathered.reshape(rows, -1)

    def from_four(array, offsets):
        groups = [
            [base ^ offset for offset in offsets]
            for base in range(blocks)
            if base == min(base ^ offset for offset in offsets)
        ]
        copies = jnp.broadcast_to(array[None], (4, *array.shape))
        return lax.all_to_all(copies, "seq", split_axis=0, concat_axis=0, axis_index_groups=groups)

    chosen = [
        (partners[0] == jnp.bitwise_xor(block_index, 1 << bit)).astype(jnp.float32) for bit in range(bits)
    ]
    bias = jnp.concatenate(
        [jnp.zeros_like(anchor_bias)[None], jnp.stack(chosen) @ level_bias.T, anchor_bias[None]], axis=0
    )

    kv_shard = jnp.concatenate([by_head(keys), by_head(values)], axis=2)
    shard5, shard4 = swap(kv_shard, 32), swap(kv_shard, 16)
    qkv = to_heads(jnp.concatenate([by_head(queries), kv_shard], axis=2))
    kv = qkv[:, places * HD :]

    token_index = block_index * rows + jnp.arange(rows, dtype=jnp.int32)
    selector = (anchor_positions[:, None] == token_index[None, :]).astype(jnp.bfloat16)
    held = jnp.dot(selector, kv, preferred_element_type=jnp.float32).astype(jnp.bfloat16)
    near, level1 = swap(kv, 1), swap(kv, 2)
    plane = jnp.sum(from_four(held, (0, 1, 2, 3)), axis=0)
    state = attend(
        None,
        qkv,
        [(rows, qkv, places, qkv, places + 1), (rows, near, 0, near, 1), (rows, level1, 0, level1, 1)],
        bias[0:3],
    )
    carried = jnp.concatenate([kv, plane], axis=0)
    level3, level2, diagonal = swap(carried, 8), swap(carried, 4), swap(carried[rows:], 12)
    shard4, shard5, state, diagonal = after((shard4, shard5, state, diagonal))
    far = to_heads(jnp.concatenate([shard4, shard5], axis=2))
    mine = plane + level2[rows:] + level3[rows:] + diagonal
    anchors = mine + swap(mine, 16) + swap(mine, 32) + swap(mine, 48)
    count = anchors.shape[0]
    result = attend(
        state,
        qkv,
        [
            (rows, level2, 0, level2, 1),
            (rows, level3, 0, level3, 1),
            (rows, far, 0, far, 1),
            (rows, far, 2, far, 3),
            (count, anchors, 0, anchors, 1),
        ],
        bias[3:8],
        final=True,
    )
    return lax.all_to_all(result, "head", split_axis=0, concat_axis=1, tiled=True)


def solution(mesh):
    in_specs = (
        P(("seq", "head"), None),
        P(("seq", "head"), None),
        P(("seq", "head"), None),
        P("head", None),
        P("head"),
        P("seq", None),
        P(),
    )
    out_specs = P(("seq", "head"), None)
    return jax.shard_map(
        on_device, mesh=mesh, in_specs=in_specs, out_specs=out_specs, check_vma=False
    )
```

```python
import functools
import math

import jax
import jax.numpy as jnp
from jax import lax
from jax.experimental import pallas as pl
from jax.experimental.pallas import tpu as pltpu
from jax.sharding import PartitionSpec as P

HD = 128
LOG2E = math.log2(math.e)


def swap(value, bit):
    return lax.ppermute(value, "seq", [(i, i ^ bit) for i in range(lax.axis_size("seq"))])


def attend_kernel(count, first, final, bias_ref, q_ref, *refs):
    k_refs, v_refs, refs = refs[: 2 * count : 2], refs[1 : 2 * count : 2], refs[2 * count :]
    refs, turned = refs[:-count], refs[-count:]
    if not first:
        acc_in, stat_in, refs = refs[0], refs[1], refs[2:]
    scale = HD**-0.5 * LOG2E
    rows, heads = q_ref.shape[0], q_ref.shape[1] // HD
    tile = 512
    for j in range(count):
        turned[j][...] = k_refs[j][...].T
    for head in range(heads):
        for start in range(0, rows, tile):
            part, cols = pl.ds(start, tile), pl.ds(head * HD, HD)
            query = q_ref[part, cols]
            scores, top = [], None
            for j in range(count):
                s = lax.dot_general(
                    query, turned[j][...], (((1,), (0,)), ((), ())), preferred_element_type=jnp.float32
                )
                bias = bias_ref[j, head] * LOG2E
                most = jnp.max(s, axis=-1, keepdims=True) * scale + bias
                top = most if top is None else jnp.maximum(top, most)
                scores.append((s, bias))
            if first:
                top = jnp.broadcast_to(top, (tile, HD))
            else:
                old_top = jnp.broadcast_to(stat_in[part, head : head + 1], (tile, HD))
                top = jnp.maximum(old_top, top)
            total = None
            for j in range(count):
                s, bias = scores[j]
                weights = jnp.exp2(s * scale - (top[:, :1] - bias)).astype(jnp.bfloat16)
                value = v_refs[j][...]
                widened = jnp.concatenate([value, jnp.ones_like(value)], axis=1)
                update = jnp.dot(weights, widened, preferred_element_type=jnp.float32)
                total = update if total is None else total + update
            acc, summed = total[:, :HD], total[:, HD:]
            if not first:
                rescale = jnp.exp2(old_top - top)
                acc = acc + acc_in[part, cols] * rescale
                old_sum = stat_in[part, heads + head : heads + head + 1]
                summed = summed + jnp.broadcast_to(old_sum, (tile, HD)) * rescale
            if final:
                refs[0][part, cols] = (acc / summed).astype(jnp.bfloat16)
            else:
                refs[0][part, cols] = acc
                refs[1][part, head : head + 1] = top[:, :1]
                refs[1][part, heads + head : heads + head + 1] = summed[:, :1]


def attend(state, queries, blocks, biases, final=False):
    rows, heads = queries.shape[0], biases.shape[1]
    width, count, first = heads * HD, len(blocks), state is None

    def whole(columns):
        return pl.BlockSpec((rows, columns), lambda i: (0, 0))

    def columns_at(size, place):
        return pl.BlockSpec((size, HD), lambda i: (0, place))

    state_specs = (whole(width), whole(2 * heads))
    in_specs = [pl.BlockSpec(memory_space=pltpu.SMEM), whole(width)]
    args = [biases, queries]
    for size, key_array, key_place, value_array, value_place in blocks:
        in_specs += [columns_at(size, key_place), columns_at(size, value_place)]
        args += [key_array, value_array]
    if not first:
        in_specs += state_specs
        args += state
    if final:
        out_shape, out_specs = jax.ShapeDtypeStruct((rows, width), jnp.bfloat16), whole(width)
    else:
        out_shape = tuple(jax.ShapeDtypeStruct((rows, n), jnp.float32) for n in (width, 2 * heads))
        out_specs = state_specs
    return pl.pallas_call(
        functools.partial(attend_kernel, count, first, final),
        grid=(1,),
        in_specs=in_specs,
        out_specs=out_specs,
        out_shape=out_shape,
        scratch_shapes=[pltpu.VMEM((HD, block[0]), jnp.bfloat16) for block in blocks],
        compiler_params=pltpu.CompilerParams(vmem_limit_bytes=24 * 1024 * 1024),
    )(*args)


def on_device(queries, keys, values, level_bias, anchor_bias, partners, anchor_positions):
    tokens = queries.shape[0]
    shards = lax.axis_size("head")
    blocks = lax.axis_size("seq")
    block_index = lax.axis_index("seq")
    bits = blocks.bit_length() - 1
    after = lax.optimization_barrier
    places = queries.shape[1] // shards // HD
    rows = shards * tokens

    def by_head(array):
        return array.reshape(tokens, shards, -1).transpose(1, 0, 2)

    def to_heads(array):
        gathered = lax.all_to_all(array, "head", split_axis=0, concat_axis=0, tiled=True)
        return gathered.reshape(rows, -1)

    def from_four(array, offsets):
        groups = [
            [base ^ offset for offset in offsets]
            for base in range(blocks)
            if base == min(base ^ offset for offset in offsets)
        ]
        copies = jnp.broadcast_to(array[None], (4, *array.shape))
        return lax.all_to_all(copies, "seq", split_axis=0, concat_axis=0, axis_index_groups=groups)

    chosen = [
        (partners[0] == jnp.bitwise_xor(block_index, 1 << bit)).astype(jnp.float32) for bit in range(bits)
    ]
    bias = jnp.concatenate(
        [
            jnp.zeros_like(anchor_bias)[None],
            jnp.sum(jnp.stack(chosen)[:, None, :] * level_bias[None], axis=2),
            anchor_bias[None],
        ],
        axis=0,
    )

    kv_shard = jnp.concatenate([by_head(keys), by_head(values)], axis=2)
    shard5, shard4 = swap(kv_shard, 32), swap(kv_shard, 16)
    qkv = to_heads(jnp.concatenate([by_head(queries), kv_shard], axis=2))
    kv = qkv[:, places * HD :]

    token_index = block_index * rows + jnp.arange(rows, dtype=jnp.int32)
    selector = (anchor_positions[:, None] == token_index[None, :]).astype(jnp.bfloat16)
    held = jnp.dot(selector, kv, preferred_element_type=jnp.float32).astype(jnp.bfloat16)
    near, level1 = swap(kv, 1), swap(kv, 2)
    plane = jnp.sum(from_four(held, (0, 1, 2, 3)), axis=0)
    state = attend(
        None,
        qkv,
        [(rows, qkv, places, qkv, places + 1), (rows, near, 0, near, 1), (rows, level1, 0, level1, 1)],
        bias[0:3],
    )
    carried = jnp.concatenate([kv, plane], axis=0)
    level3, level2, diagonal = swap(carried, 8), swap(carried, 4), swap(carried[rows:], 12)
    shard5, shard4, state = after((shard5, shard4, state))
    far = to_heads(jnp.concatenate([shard4, shard5], axis=2))
    mine = plane + level2[rows:] + level3[rows:] + diagonal
    anchors = mine + swap(mine, 16) + swap(mine, 32) + swap(mine, 48)
    count = anchors.shape[0]
    result = attend(
        state,
        qkv,
        [
            (rows, level2, 0, level2, 1),
            (rows, level3, 0, level3, 1),
            (rows, far, 0, far, 1),
            (rows, far, 2, far, 3),
            (count, anchors, 0, anchors, 1),
        ],
        bias[3:8],
        final=True,
    )
    return lax.all_to_all(result, "head", split_axis=0, concat_axis=1, tiled=True)


def solution(mesh):
    in_specs = (
        P(("seq", "head"), None),
        P(("seq", "head"), None),
        P(("seq", "head"), None),
        P("head", None),
        P("head"),
        P("seq", None),
        P(),
    )
    out_specs = P(("seq", "head"), None)
    return jax.shard_map(
        on_device, mesh=mesh, in_specs=in_specs, out_specs=out_specs, check_vma=False
    )
```

```python
import functools
import math

import jax
import jax.numpy as jnp
from jax import lax
from jax.experimental import pallas as pl
from jax.experimental.pallas import tpu as pltpu
from jax.sharding import PartitionSpec as P

HD = 128
LOG2E = math.log2(math.e)


def swap(value, bit):
    return lax.ppermute(value, "seq", [(i, i ^ bit) for i in range(lax.axis_size("seq"))])


def attend_kernel(count, first, final, bias_ref, q_ref, *refs):
    k_refs, v_refs, refs = refs[: 2 * count : 2], refs[1 : 2 * count : 2], refs[2 * count :]
    refs, turned = refs[:-count], refs[-count:]
    if not first:
        acc_in, stat_in, refs = refs[0], refs[1], refs[2:]
    scale = HD**-0.5 * LOG2E
    rows, heads = q_ref.shape[0], q_ref.shape[1] // HD
    tile = 512
    for j in range(count):
        turned[j][...] = k_refs[j][...].T
    for head in range(heads):
        for start in range(0, rows, tile):
            part, cols = pl.ds(start, tile), pl.ds(head * HD, HD)
            query = q_ref[part, cols]
            scores, top = [], None
            for j in range(count):
                s = lax.dot_general(
                    query, turned[j][...], (((1,), (0,)), ((), ())), preferred_element_type=jnp.float32
                )
                bias = bias_ref[j, head] * LOG2E
                most = jnp.max(s, axis=-1, keepdims=True) * scale + bias
                top = most if top is None else jnp.maximum(top, most)
                scores.append((s, bias))
            if first:
                top = jnp.broadcast_to(top, (tile, HD))
            else:
                old_top = jnp.broadcast_to(stat_in[part, head : head + 1], (tile, HD))
                top = jnp.maximum(old_top, top)
            total = None
            for j in range(count):
                s, bias = scores[j]
                weights = jnp.exp2(s * scale - (top[:, :1] - bias)).astype(jnp.bfloat16)
                value = v_refs[j][...]
                widened = jnp.concatenate([value, jnp.ones_like(value)], axis=1)
                update = jnp.dot(weights, widened, preferred_element_type=jnp.float32)
                total = update if total is None else total + update
            acc, summed = total[:, :HD], total[:, HD:]
            if not first:
                rescale = jnp.exp2(old_top - top)
                acc = acc + acc_in[part, cols] * rescale
                old_sum = stat_in[part, heads + head : heads + head + 1]
                summed = summed + jnp.broadcast_to(old_sum, (tile, HD)) * rescale
            if final:
                refs[0][part, cols] = (acc / summed).astype(jnp.bfloat16)
            else:
                refs[0][part, cols] = acc
                refs[1][part, head : head + 1] = top[:, :1]
                refs[1][part, heads + head : heads + head + 1] = summed[:, :1]


def attend(state, queries, blocks, biases, final=False):
    rows, heads = queries.shape[0], biases.shape[1]
    width, count, first = heads * HD, len(blocks), state is None

    def whole(columns):
        return pl.BlockSpec((rows, columns), lambda i: (0, 0))

    def columns_at(size, place):
        return pl.BlockSpec((size, HD), lambda i: (0, place))

    state_specs = (whole(width), whole(2 * heads))
    in_specs = [pl.BlockSpec(memory_space=pltpu.SMEM), whole(width)]
    args = [biases, queries]
    for size, key_array, key_place, value_array, value_place in blocks:
        in_specs += [columns_at(size, key_place), columns_at(size, value_place)]
        args += [key_array, value_array]
    if not first:
        in_specs += state_specs
        args += state
    if final:
        out_shape, out_specs = jax.ShapeDtypeStruct((rows, width), jnp.bfloat16), whole(width)
    else:
        out_shape = tuple(jax.ShapeDtypeStruct((rows, n), jnp.float32) for n in (width, 2 * heads))
        out_specs = state_specs
    return pl.pallas_call(
        functools.partial(attend_kernel, count, first, final),
        grid=(1,),
        in_specs=in_specs,
        out_specs=out_specs,
        out_shape=out_shape,
        scratch_shapes=[pltpu.VMEM((HD, block[0]), jnp.bfloat16) for block in blocks],
        compiler_params=pltpu.CompilerParams(vmem_limit_bytes=24 * 1024 * 1024),
    )(*args)


def on_device(queries, keys, values, level_bias, anchor_bias, partners, anchor_positions):
    tokens = queries.shape[0]
    shards = lax.axis_size("head")
    blocks = lax.axis_size("seq")
    block_index = lax.axis_index("seq")
    bits = blocks.bit_length() - 1
    after = lax.optimization_barrier
    places = queries.shape[1] // shards // HD
    rows = shards * tokens

    def by_head(array):
        return array.reshape(tokens, shards, -1).transpose(1, 0, 2)

    def to_heads(array):
        gathered = lax.all_to_all(array, "head", split_axis=0, concat_axis=0, tiled=True)
        return gathered.reshape(rows, -1)

    def from_four(array, offsets):
        groups = [
            [base ^ offset for offset in offsets]
            for base in range(blocks)
            if base == min(base ^ offset for offset in offsets)
        ]
        copies = jnp.broadcast_to(array[None], (4, *array.shape))
        return lax.all_to_all(copies, "seq", split_axis=0, concat_axis=0, axis_index_groups=groups)

    chosen = [
        (partners[0] == jnp.bitwise_xor(block_index, 1 << bit)).astype(jnp.float32) for bit in range(bits)
    ]
    bias = jnp.concatenate(
        [
            jnp.zeros_like(anchor_bias)[None],
            jnp.sum(jnp.stack(chosen)[:, None, :] * level_bias[None], axis=2),
            anchor_bias[None],
        ],
        axis=0,
    )

    kv_shard = jnp.concatenate([by_head(keys), by_head(values)], axis=2)
    shard5, shard4 = swap(kv_shard, 32), swap(kv_shard, 16)
    qkv = to_heads(jnp.concatenate([by_head(queries), kv_shard], axis=2))
    kv = qkv[:, places * HD :]

    token_index = block_index * rows + jnp.arange(rows, dtype=jnp.int32)
    selector = (anchor_positions[:, None] == token_index[None, :]).astype(jnp.bfloat16)
    held = jnp.dot(selector, kv, preferred_element_type=jnp.float32).astype(jnp.bfloat16)
    near, level1 = swap(kv, 1), swap(kv, 2)
    plane = jnp.sum(from_four(held, (0, 1, 2, 3)), axis=0)
    state = attend(
        None,
        qkv,
        [(rows, qkv, places, qkv, places + 1), (rows, near, 0, near, 1), (rows, level1, 0, level1, 1)],
        bias[0:3],
    )
    plane16, plane32, plane48 = swap(plane, 16), swap(plane, 32), swap(plane, 48)
    kv_2, plane = after((kv, plane))
    level3, level2 = swap(kv_2, 8), swap(kv_2, 4)
    shard4, shard5, state, plane48, plane32, plane16 = after(
        (shard4, shard5, state, plane48, plane32, plane16)
    )
    far = to_heads(jnp.concatenate([shard4, shard5], axis=2))
    strided = plane + plane16 + plane32 + plane48
    strided, level2, level3 = after((strided, level2, level3))
    anchors = strided + swap(strided, 4) + swap(strided, 8) + swap(strided, 12)
    count = anchors.shape[0]
    result = attend(
        state,
        qkv,
        [
            (rows, level2, 0, level2, 1),
            (rows, level3, 0, level3, 1),
            (rows, far, 0, far, 1),
            (rows, far, 2, far, 3),
            (count, anchors, 0, anchors, 1),
        ],
        bias[3:8],
        final=True,
    )
    return lax.all_to_all(result, "head", split_axis=0, concat_axis=1, tiled=True)


def solution(mesh):
    in_specs = (
        P(("seq", "head"), None),
        P(("seq", "head"), None),
        P(("seq", "head"), None),
        P("head", None),
        P("head"),
        P("seq", None),
        P(),
    )
    out_specs = P(("seq", "head"), None)
    return jax.shard_map(
        on_device, mesh=mesh, in_specs=in_specs, out_specs=out_specs, check_vma=False
    )
```

```python
import functools
import math

import jax
import jax.numpy as jnp
from jax import lax
from jax.experimental import pallas as pl
from jax.experimental.pallas import tpu as pltpu
from jax.sharding import PartitionSpec as P

HD = 128
LOG2E = math.log2(math.e)


def swap(value, bit):
    return lax.ppermute(value, "seq", [(i, i ^ bit) for i in range(lax.axis_size("seq"))])


def attend_kernel(count, first, final, bias_ref, q_ref, *refs):
    k_refs, v_refs, refs = refs[: 2 * count : 2], refs[1 : 2 * count : 2], refs[2 * count :]
    refs, turned = refs[:-count], refs[-count:]
    if not first:
        acc_in, stat_in, refs = refs[0], refs[1], refs[2:]
    scale = HD**-0.5 * LOG2E
    rows, heads = q_ref.shape[0], q_ref.shape[1] // HD
    tile = 512
    for j in range(count):
        turned[j][...] = k_refs[j][...].T
    for head in range(heads):
        for start in range(0, rows, tile):
            part, cols = pl.ds(start, tile), pl.ds(head * HD, HD)
            query = q_ref[part, cols]
            scores, top = [], None
            for j in range(count):
                s = lax.dot_general(
                    query, turned[j][...], (((1,), (0,)), ((), ())), preferred_element_type=jnp.float32
                )
                bias = bias_ref[j, head] * LOG2E
                most = jnp.max(s, axis=-1, keepdims=True) * scale + bias
                top = most if top is None else jnp.maximum(top, most)
                scores.append((s, bias))
            if first:
                top = jnp.broadcast_to(top, (tile, HD))
            else:
                old_top = jnp.broadcast_to(stat_in[part, head : head + 1], (tile, HD))
                top = jnp.maximum(old_top, top)
            total = None
            for j in range(count):
                s, bias = scores[j]
                weights = jnp.exp2(s * scale - (top[:, :1] - bias)).astype(jnp.bfloat16)
                value = v_refs[j][...]
                widened = jnp.concatenate([value, jnp.ones_like(value)], axis=1)
                update = jnp.dot(weights, widened, preferred_element_type=jnp.float32)
                total = update if total is None else total + update
            acc, summed = total[:, :HD], total[:, HD:]
            if not first:
                rescale = jnp.exp2(old_top - top)
                acc = acc + acc_in[part, cols] * rescale
                old_sum = stat_in[part, heads + head : heads + head + 1]
                summed = summed + jnp.broadcast_to(old_sum, (tile, HD)) * rescale
            if final:
                refs[0][part, cols] = (acc / summed).astype(jnp.bfloat16)
            else:
                refs[0][part, cols] = acc
                refs[1][part, head : head + 1] = top[:, :1]
                refs[1][part, heads + head : heads + head + 1] = summed[:, :1]


def attend(state, queries, blocks, biases, final=False):
    rows, heads = queries.shape[0], biases.shape[1]
    width, count, first = heads * HD, len(blocks), state is None

    def whole(columns):
        return pl.BlockSpec((rows, columns), lambda i: (0, 0))

    def columns_at(size, place):
        return pl.BlockSpec((size, HD), lambda i: (0, place))

    state_specs = (whole(width), whole(2 * heads))
    in_specs = [pl.BlockSpec(memory_space=pltpu.SMEM), whole(width)]
    args = [biases, queries]
    for size, key_array, key_place, value_array, value_place in blocks:
        in_specs += [columns_at(size, key_place), columns_at(size, value_place)]
        args += [key_array, value_array]
    if not first:
        in_specs += state_specs
        args += state
    if final:
        out_shape, out_specs = jax.ShapeDtypeStruct((rows, width), jnp.bfloat16), whole(width)
    else:
        out_shape = tuple(jax.ShapeDtypeStruct((rows, n), jnp.float32) for n in (width, 2 * heads))
        out_specs = state_specs
    return pl.pallas_call(
        functools.partial(attend_kernel, count, first, final),
        grid=(1,),
        in_specs=in_specs,
        out_specs=out_specs,
        out_shape=out_shape,
        scratch_shapes=[pltpu.VMEM((HD, block[0]), jnp.bfloat16) for block in blocks],
        compiler_params=pltpu.CompilerParams(vmem_limit_bytes=24 * 1024 * 1024),
    )(*args)


def on_device(queries, keys, values, level_bias, anchor_bias, partners, anchor_positions):
    tokens = queries.shape[0]
    shards = lax.axis_size("head")
    blocks = lax.axis_size("seq")
    block_index = lax.axis_index("seq")
    bits = blocks.bit_length() - 1
    after = lax.optimization_barrier
    places = queries.shape[1] // shards // HD
    rows = shards * tokens

    def by_head(array):
        return array.reshape(tokens, shards, -1).transpose(1, 0, 2)

    def to_heads(array):
        gathered = lax.all_to_all(array, "head", split_axis=0, concat_axis=0, tiled=True)
        return gathered.reshape(rows, -1)

    def from_four(array, offsets):
        groups = [
            [base ^ offset for offset in offsets]
            for base in range(blocks)
            if base == min(base ^ offset for offset in offsets)
        ]
        copies = jnp.broadcast_to(array[None], (4, *array.shape))
        return lax.all_to_all(copies, "seq", split_axis=0, concat_axis=0, axis_index_groups=groups)

    chosen = [
        (partners[0] == jnp.bitwise_xor(block_index, 1 << bit)).astype(jnp.float32) for bit in range(bits)
    ]
    bias = jnp.concatenate(
        [
            jnp.zeros_like(anchor_bias)[None],
            jnp.sum(jnp.stack(chosen)[:, None, :] * level_bias[None], axis=2),
            anchor_bias[None],
        ],
        axis=0,
    )

    kv_shard = jnp.concatenate([by_head(keys), by_head(values)], axis=2)
    shard5, shard4 = swap(kv_shard, 32), swap(kv_shard, 16)
    qkv = to_heads(jnp.concatenate([by_head(queries), kv_shard], axis=2))
    kv = qkv[:, places * HD :]

    token_index = block_index * rows + jnp.arange(rows, dtype=jnp.int32)
    selector = (anchor_positions[:, None] == token_index[None, :]).astype(jnp.bfloat16)
    held = jnp.dot(selector, kv, preferred_element_type=jnp.float32).astype(jnp.bfloat16)
    near, level1 = swap(kv, 1), swap(kv, 2)
    plane = jnp.sum(from_four(held, (0, 1, 2, 3)), axis=0)
    state = attend(
        None,
        qkv,
        [(rows, qkv, places, qkv, places + 1), (rows, near, 0, near, 1), (rows, level1, 0, level1, 1)],
        bias[0:3],
    )
    plane16, plane32, plane48 = swap(plane, 16), swap(plane, 32), swap(plane, 48)
    kv_2, plane = after((kv, plane))
    level3, level2 = swap(kv_2, 8), swap(kv_2, 4)
    shard4, shard5, state, plane48, plane32, plane16 = after(
        (shard4, shard5, state, plane48, plane32, plane16)
    )
    far = to_heads(jnp.concatenate([shard4, shard5], axis=2))
    strided = plane + plane16 + plane32 + plane48
    strided, level3 = after((strided, level3))
    anchors = strided + swap(strided, 4) + swap(strided, 8) + swap(strided, 12)
    count = anchors.shape[0]
    result = attend(
        state,
        qkv,
        [
            (rows, level2, 0, level2, 1),
            (rows, level3, 0, level3, 1),
            (rows, far, 0, far, 1),
            (rows, far, 2, far, 3),
            (count, anchors, 0, anchors, 1),
        ],
        bias[3:8],
        final=True,
    )
    return lax.all_to_all(result, "head", split_axis=0, concat_axis=1, tiled=True)


def solution(mesh):
    in_specs = (
        P(("seq", "head"), None),
        P(("seq", "head"), None),
        P(("seq", "head"), None),
        P("head", None),
        P("head"),
        P("seq", None),
        P(),
    )
    out_specs = P(("seq", "head"), None)
    return jax.shard_map(
        on_device, mesh=mesh, in_specs=in_specs, out_specs=out_specs, check_vma=False
    )
```
